256 devices in a mesh: region: 64 (over x, z, core), ray: 4 (over y).
Axes of the slice: x: 4, y: 4, z: 8, core: 2. Of those that a mesh axis runs over, the one named last changes fastest.
Arguments:
- bricks: bfloat16 [64, 512, 512], P('region', 'ray'), may hold values from -6 to 6
- pair_index: int32 [64, 256, 16], P('region', 'ray'), may hold values from 0 to 511
- interp_weight: bfloat16 [64, 256, 512, 128], P('region', 'ray'), may hold values from 0 to 0.15234375
- step_len: float32 [64, 2, 65536], P('region', None, 'ray'), may hold values from 0.00234375 to 0.09375
- sample_count: int32 [64, 65536], P('region', 'ray'), may hold values from 0 to 2
- w_first: bfloat16 [64, 256], replicated, may hold values from -0.75 to 0.75
- w_second: bfloat16 [256, 256], replicated, may hold values from -0.375 to 0.375
- w_out: bfloat16 [256, 33], replicated, may hold values from -0.375 to 0.375
Outputs:
- color: float32 [32, 65536], P(None, ('ray', 'region'))
- transmittance: float32 [65536], P(('ray', 'region'))
The draws below stay inside these ranges and needn't reach their ends.
All inputs are finite; a program needn't handle non-finite values.
Results may differ from the reference program's by a relative error of at most 0.0015.
Values may be sent and summed in bfloat16 or wider, within the bound.
A program may use at most 128 MiB of HBM per device.

```python
import math
from functools import partial
import jax
import jax.numpy as jnp
from jax import lax

C = 64
HID = 256
FEAT = 32
BV = 8
P_SIZE = 16
TR = 256
SAMP = 2
SLABS = 64
NB = 512
RAYS = 65536
TILES = 256


def plant(values, rng, smallest, top_value):
    longest = values.shape.index(max(values.shape))
    spots = []
    for shift in (0, 1):
        where = [jax.random.randint(jax.random.fold_in(rng, axis), (), 0, length) for axis, length in enumerate(values.shape)]
        where[longest] = (where[longest] + shift) % values.shape[longest]
        spots.append(tuple(where))
    return values.at[spots[0]].set(smallest).at[spots[1]].set(top_value)


def level_of(stream_key, shape, shards, least, largest):
    factor_of = 1.0
    for dim, blocks in shards:
        draws = jax.random.uniform(jax.random.fold_in(jax.random.fold_in(stream_key, 6), dim), (blocks,), jnp.float32, least / len(shards), largest / len(shards))
        factor_of = factor_of * jnp.repeat(jnp.exp(draws), shape[dim] // blocks).reshape((-1,) + (1,) * (len(shape) - 1 - dim))
    return factor_of


def gaussian(stream_key, extent, width, bound, split=(), kind=jnp.bfloat16):
    gain = level_of(stream_key, extent, split, -0.22, 0.18) if split else 1.0
    result = jax.random.normal(stream_key, extent, jnp.float32) * width * gain
    return jnp.minimum(jnp.maximum(result, -bound), bound).astype(kind)


def setup_inputs(seed: int = 0) -> dict:
    splits = jax.random.split(jax.random.key(seed), 9)
    return {
        "bricks": gaussian(splits[0], (SLABS, NB, BV * C), 1.0, 6.0, ((0, 64), (1, 4))),
        "pair_index": plant(jax.random.randint(splits[1], (SLABS, TILES, P_SIZE), 0, NB), jax.random.fold_in(splits[1], 1), 0, NB - 1).astype(jnp.int32),
        "interp_weight": jnp.clip(0.15234375 * jax.random.uniform(splits[2], (SLABS, TILES, TR * SAMP, P_SIZE * BV), jnp.float32) ** level_of(splits[2], (SLABS, TILES, TR * SAMP, P_SIZE * BV), ((0, 64), (1, 4)), -0.2, 0.2), 0.0, 0.15234375).astype(jnp.bfloat16),
        "step_len": jnp.clip(jnp.exp(math.log(0.09375) - 3.6888794 * jax.random.uniform(splits[3], (SLABS, SAMP, RAYS), jnp.float32) ** level_of(splits[3], (SLABS, SAMP, RAYS), ((0, 64), (2, 4)), -0.2, 0.2)), 0.00234375, 0.09375),
        "sample_count": plant(jax.random.randint(splits[4], (SLABS, RAYS), 0, SAMP + 1), jax.random.fold_in(splits[4], 1), 0, SAMP).astype(jnp.int32),
        "w_first": gaussian(splits[5], (C, HID), C ** -0.5, 0.75),
        "w_second": gaussian(splits[6], (HID, HID), HID ** -0.5, 0.375),
        "w_out": gaussian(splits[7], (HID, FEAT + 1), HID ** -0.5, 0.375),
    }


def shade(field, steps, counts):
    nfeat = field.shape[0] - 1
    feats = field[:nfeat]
    sigma = jax.nn.softplus(field[nfeat])
    depth = steps.shape[1]
    live = (jnp.arange(depth, dtype=jnp.int32)[None, :] < counts[:, None]).astype(jnp.float32)
    tau = sigma * steps * live
    before = jnp.cumsum(tau, axis=1) - tau
    weights = jnp.exp(-before) * (1.0 - jnp.exp(-tau))
    slab_color = jnp.sum(feats * weights[None, :, :], axis=2)
    slab_trans = jnp.exp(-jnp.sum(tau, axis=1))
    return slab_color, slab_trans


def dot32(form, a, b):
    return jnp.einsum(form, a.astype(jnp.float32), b.astype(jnp.float32), precision=lax.Precision.HIGHEST)


def one_slab(items, w_first, w_second, w_out):
    table, index, weight, steps, counts = items
    channels = C
    tiles = index.shape[0]
    rows = jnp.take(table, index.reshape(-1), axis=0).reshape(tiles, P_SIZE * BV, channels)
    feats = dot32('tsk,tkc->cts', weight, rows).astype(jnp.bfloat16).reshape(channels, -1)
    first = jax.nn.relu(dot32('ch,cs->hs', w_first, feats)).astype(jnp.bfloat16)
    second = jax.nn.relu(dot32('hg,hs->gs', w_second, first)).astype(jnp.bfloat16)
    field = dot32('hf,hs->fs', w_out, second)
    rays = steps.shape[1]
    field = field.reshape(field.shape[0], rays, SAMP)
    return shade(field, steps.T, counts)


def reference(bricks, pair_index, interp_weight, step_len, sample_count, w_first, w_second, w_out):
    slab_fn = partial(one_slab, w_first=w_first, w_second=w_second, w_out=w_out)
    colors, trans = lax.map(slab_fn, (bricks, pair_index, interp_weight, step_len, sample_count))
    ahead = jnp.cumprod(trans, axis=0)
    before = jnp.concatenate([jnp.ones((1, trans.shape[1]), jnp.float32), ahead[:-1]], axis=0)
    color = jnp.sum(before[:, None, :] * colors, axis=0)
    return color, ahead[-1]
```

```python
import functools

import jax
import jax.numpy as jnp
from jax import lax
from jax.experimental import pallas as pl
from jax.experimental.pallas import tpu as pltpu
from jax.sharding import PartitionSpec as P

BF = jnp.bfloat16
F32 = jnp.float32
MESH = pl.DeviceIdType.MESH

NX, NZ, NY = 4, 8, 4
TILES = 64
RAYS = 256
LANES = 128
GROUP = 4
STEPS = TILES // GROUP
ROWS = 72
USED = 66
CHUNKS = 8


def softplus(x):
    return jnp.maximum(x, 0.0) + jnp.log1p(jnp.exp(-jnp.abs(x)))


def put(ref, color, light):
    ref[0:32, :] = color[:, :LANES]
    ref[32:64, :] = color[:, LANES:]
    ref[64:65, :] = light[:, :LANES]
    ref[65:66, :] = light[:, LANES:]


def get(ref):
    return ref[0:32, :], ref[32:64, :], ref[64:65, :], ref[65:66, :]


def ordered(pieces):
    left, right, tleft, tright = pieces[0]
    for a, b, ta, tb in pieces[1:]:
        left = left + tleft * a
        right = right + tright * b
        tleft = tleft * ta
        tright = tright * tb
    return left, right, tleft, tright


def put4(ref, piece):
    ref[0:32, :] = piece[0]
    ref[32:64, :] = piece[1]
    ref[64:65, :] = piece[2]
    ref[65:66, :] = piece[3]


def kernel(
    bricks, index_hbm, interp, step_hbm, count_hbm, w1_hbm, w2_hbm, wo_hbm,
    color_out, light_out,
    table_bf, index, wv, step, count, w1, w2, wo, w2t,
    stage, table, h1a, h1b, h2a, h2b,
    mine, csend, crecv, zsend, zrecv, xsend, xrecv,
    in_sem, wv_sem, ysend_sem, yrecv_sem, cs_sem, cr_sem, zs_sem, zr_sem, xs_sem, xr_sem,
):
    region = lax.axis_index("region")
    y = lax.axis_index("ray")
    core = lax.rem(region, 2)
    z = lax.rem(region // 2, NZ)
    x = region // (2 * NZ)

    def at(px, pz, pc):
        return {"region": px * (2 * NZ) + pz * 2 + pc}

    small = [
        pltpu.make_async_copy(src, dst, in_sem.at[i])
        for i, (src, dst) in enumerate(
            [
                (w1_hbm, w1), (w2_hbm, w2), (wo_hbm, wo), (index_hbm.at[0], index),
                (step_hbm.at[0], step), (count_hbm, count),
                (bricks.at[0], table_bf.at[pl.ds(y * 128, 128)]),
            ]
        )
    ]
    for copy in small:
        copy.start()

    def wv_copy(c):
        n = TILES // CHUNKS
        return pltpu.make_async_copy(interp.at[0, pl.ds(c * n, n)], wv.at[pl.ds(c * n, n)], wv_sem.at[c])

    for c in range(CHUNKS):
        wv_copy(c).start()

    barrier = pltpu.get_barrier_semaphore()

    def hello(device):
        pl.semaphore_signal(barrier, inc=1, device_id=device, device_id_type=MESH)

    for d in range(1, NY):
        hello({"ray": lax.rem(y + d, NY)})
    hello(at(x, z, 1 - core))
    for d in range(1, NZ):
        hello(at(x, lax.rem(z + d, NZ), core))
    for d in range(1, NX):
        hello(at(lax.rem(x + d, NX), z, core))
    pl.semaphore_wait(barrier, (NY - 1) + 1 + (NZ - 1) + (NX - 1))

    def y_copy(d):
        return pltpu.make_async_remote_copy(
            src_ref=bricks.at[0],
            dst_ref=table_bf.at[pl.ds(y * 128, 128)],
            send_sem=ysend_sem.at[d],
            recv_sem=yrecv_sem.at[d],
            device_id={"ray": lax.rem(y + d, NY)},
            device_id_type=MESH,
        )

    for d in (1, 3, 2):
        y_copy(d).start()

    for copy in small:
        copy.wait()
    w2t[...] = w2[...].astype(F32).T.astype(BF)

    for c in range(CHUNKS):
        wv_copy(c).wait()

        @pl.loop(0, TILES // CHUNKS)
        def _(i):
            t = c * (TILES // CHUNKS) + i
            b = lax.rem(i, 2)
            stage[b] = wv[t].astype(F32)
            wv[t, 0:RAYS] = stage[b, pl.ds(0, RAYS, stride=2), :].astype(BF)
            wv[t, RAYS : 2 * RAYS] = stage[b, pl.ds(1, RAYS, stride=2), :].astype(BF)

    for d in range(1, NY):
        y_copy(d).wait()

    half = w1[...]
    none = jnp.zeros_like(half)
    wide = [jnp.concatenate([half, none], 0), jnp.concatenate([none, half], 0)]
    for v in range(8):
        cols = (v // 2) * LANES
        got = jnp.dot(table_bf[:, cols : cols + LANES], wide[v % 2], preferred_element_type=F32)
        flat = table.reshape(2, 4096, LANES)
        flat[0, pl.ds(v, 512, stride=8), :] = got[:, :LANES]
        flat[1, pl.ds(v, 512, stride=8), :] = got[:, LANES:]

    def offsets(i):
        j = lax.rem(i, 4)
        return 4 + j, 3 - j

    def column(k):
        return lax.rem(x + 1 + k, NX)

    def tile(i, u):
        off = offsets(i)[u % 2]
        c = core if u < 2 else 1 - core
        return column(i // 4) * (2 * NZ) + lax.rem(z + off, NZ) * 2 + c

    def layer1(i, h1):
        for u in range(GROUP):
            t = tile(i, u)
            ids = [index[j, t] for j in range(16)]
            g = [jnp.concatenate([table[h, b] for b in ids], 0).T for h in range(2)]
            g = jnp.concatenate(g, 0).astype(BF)
            r = lax.dot_general(g, wv[t], (((1,), (1,)), ((), ())), preferred_element_type=F32)
            h1[u * 256 : (u + 1) * 256] = jnp.maximum(r.astype(BF), 0)

    def layer2(h1, h2):
        for u in range(GROUP):
            r = jnp.dot(w2t[...], h1[u * 256 : (u + 1) * 256], preferred_element_type=F32)
            h2[u * 256 : (u + 1) * 256] = jnp.maximum(r.astype(BF), 0)

    def layer3(i, h2):
        for u in range(GROUP):
            t = tile(i, u)
            o = jnp.dot(wo[...], h2[u * 256 : (u + 1) * 256], preferred_element_type=F32)
            lanes = pl.ds(pl.multiple_of(t * RAYS, RAYS), RAYS)
            n = count[0:1, lanes]
            tau0 = softplus(o[32:33, :RAYS]) * step[0:1, lanes] * jnp.where(n > 0, 1.0, 0.0)
            tau1 = softplus(o[32:33, RAYS:]) * step[1:2, lanes] * jnp.where(n > 1, 1.0, 0.0)
            a0 = jnp.exp(-tau0)
            a1 = jnp.exp(-tau1)
            color = o[0:32, :RAYS] * (1.0 - a0) + o[0:32, RAYS:] * (a0 * (1.0 - a1))
            put((mine if u < 2 else csend).at[i, u % 2], color, a0 * a1)

    def c_copy(g):
        return pltpu.make_async_remote_copy(
            src_ref=csend.at[g],
            dst_ref=crecv.at[g],
            send_sem=cs_sem.at[g],
            recv_sem=cr_sem.at[g],
            device_id=at(x, z, 1 - core),
            device_id_type=MESH,
        )

    def z_copy(k, off):
        return pltpu.make_async_remote_copy(
            src_ref=zsend.at[k, off, pl.ds(0, USED)],
            dst_ref=zrecv.at[k, z, pl.ds(0, USED)],
            send_sem=zs_sem.at[k, off],
            recv_sem=zr_sem.at[k, z],
            device_id=at(x, lax.rem(z + off, NZ), core),
            device_id_type=MESH,
        )

    def z_wait(k, src):
        pltpu.make_async_copy(
            zrecv.at[k, src, pl.ds(0, USED)], zrecv.at[k, src, pl.ds(0, USED)], zr_sem.at[k, src]
        ).wait()

    def x_copy(k):
        return pltpu.make_async_remote_copy(
            src_ref=xsend.at[k, pl.ds(0, USED)],
            dst_ref=xrecv.at[x, pl.ds(0, USED)],
            send_sem=xs_sem.at[k],
            recv_sem=xr_sem.at[x],
            device_id=at(column(k), z, core),
            device_id_type=MESH,
        )

    def merge_cores(g):
        c_copy(g).wait_recv()
        front = core == 0
        k = g // 4
        off = offsets(g)
        for u in range(2):
            a, b = get(mine.at[g, u]), get(crecv.at[g, u])
            near = [jnp.where(front, p, q) for p, q in zip(a, b)]
            far = [jnp.where(front, q, p) for p, q in zip(a, b)]
            piece = ordered([near, far])
            if u == 0:
                put4(zsend.at[k, off[0]], piece)
                z_copy(k, off[0]).start()
            else:
                own = lax.rem(g, 4) == 3

                @pl.when(own)
                def _():
                    put4(zrecv.at[k, z], piece)

                @pl.when(jnp.logical_not(own))
                def _():
                    put4(zsend.at[k, off[1]], piece)
                    z_copy(k, off[1]).start()

    def merge_z(k):
        @pl.loop(1, NZ)
        def _(d):
            z_wait(k, lax.rem(z + d, NZ))

        return ordered([get(zrecv.at[k, s]) for s in range(NZ)])

    def hand_on(k):
        put4(xsend.at[k], merge_z(k))
        x_copy(k).start()

    def finish(i, h2):
        layer3(i, h2)
        c_copy(i).start()

    def work(i, now, before):
        layer3(i - 2, now[1])
        layer2(before[0], before[1])
        layer1(i, now[0])
        c_copy(i - 2).start()

        @pl.when(i >= 4)
        def _():
            merge_cores(i - 4)

        @pl.when(jnp.logical_and(i >= 11, lax.rem(i, 4) == 3))
        def _():
            hand_on((i - 11) // 4)

    even, odd = (h1a, h2a), (h1b, h2b)
    layer1(0, h1a)
    layer2(h1a, h2a)
    layer1(1, h1b)

    @pl.loop(1, STEPS // 2)
    def _(n):
        work(2 * n, even, odd)
        work(2 * n + 1, odd, even)

    layer3(STEPS - 2, h2a)
    layer2(h1b, h2b)
    c_copy(STEPS - 2).start()
    layer3(STEPS - 1, h2b)
    c_copy(STEPS - 1).start()

    @pl.loop(STEPS - 4, STEPS)
    def _(g):
        merge_cores(g)

    hand_on(2)
    put4(xrecv.at[x], merge_z(3))
    for d in range(1, NX):
        src = lax.rem(x + d, NX)
        pltpu.make_async_copy(xrecv.at[src, pl.ds(0, USED)], xrecv.at[src, pl.ds(0, USED)], xr_sem.at[src]).wait()
    left, right, tleft, tright = ordered([get(xrecv.at[s]) for s in range(NX)])
    color_out[:, :LANES] = left
    color_out[:, LANES:] = right
    light_out[:, :LANES] = tleft
    light_out[:, LANES:] = tright

    @pl.loop(0, STEPS)
    def _(g):
        c_copy(g).wait_send()
        z_copy(g // 4, offsets(g)[0]).wait_send()

        @pl.when(lax.rem(g, 4) < 3)
        def _():
            z_copy(g // 4, offsets(g)[1]).wait_send()

    for k in range(3):
        x_copy(k).wait_send()


def shards(bricks, pair_index, interp_weight, step_len, sample_count, w_first, w_second, w_out):
    part = functools.partial(pltpu.VMEM, dtype=F32)
    dma = pltpu.SemaphoreType.DMA
    color, light = pl.pallas_call(
        kernel,
        out_shape=(jax.ShapeDtypeStruct((32, RAYS), F32), jax.ShapeDtypeStruct((1, RAYS), F32)),
        in_specs=[pl.BlockSpec(memory_space=pl.ANY)] * 8,
        out_specs=[pl.BlockSpec(memory_space=pltpu.VMEM)] * 2,
        scratch_shapes=[
            pltpu.VMEM((512, 512), BF),
            pltpu.SMEM((16, 64), jnp.int32),
            pltpu.VMEM((TILES, 2 * RAYS, LANES), BF),
            pltpu.VMEM((2, TILES * RAYS), F32),
            pltpu.VMEM((1, TILES * RAYS), jnp.int32),
            pltpu.VMEM((64, 256), BF),
            pltpu.VMEM((256, 256), BF),
            pltpu.VMEM((33, 256), BF),
            pltpu.VMEM((256, 256), BF),
            pltpu.VMEM((2, 2 * RAYS, LANES), F32),
            pltpu.VMEM((2, 512, 8, LANES), F32),
        ]
        + [pltpu.VMEM((GROUP * 256, 512), BF)] * 4
        + [part((STEPS, 2, ROWS, LANES))] * 3
        + [part((NX, NZ, ROWS, LANES))] * 2
        + [part((NX, ROWS, LANES))] * 2
        + [dma((7,)), dma((CHUNKS,)), dma((NY,)), dma((NY,)), dma((STEPS,)), dma((STEPS,))]
        + [dma((NX, NZ)), dma((NX, NZ)), dma((NX,)), dma((NX,))],
        compiler_params=pltpu.CompilerParams(
            collective_id=0, has_side_effects=True, vmem_limit_bytes=50 * 2**20
        ),
        name="render",
    )(
        bricks,
        jnp.swapaxes(pair_index, 1, 2),
        interp_weight,
        step_len,
        sample_count,
        w_first,
        w_second,
        w_out.T,
    )
    return color, light.reshape(RAYS)


def solution(mesh):
    return jax.shard_map(
        shards,
        mesh=mesh,
        in_specs=(
            P("region", "ray", None),
            P("region", "ray", None),
            P("region", "ray", None, None),
            P("region", None, "ray"),
            P("region", "ray"),
            P(),
            P(),
            P(),
        ),
        out_specs=(P(None, ("ray", "region")), P(("ray", "region"))),
        check_vma=False,
    )
```

```python
import functools

import jax
import jax.numpy as jnp
from jax import lax
from jax.experimental import pallas as pl
from jax.experimental.pallas import tpu as pltpu
from jax.sharding import PartitionSpec as P

BF = jnp.bfloat16
F32 = jnp.float32
MESH = pl.DeviceIdType.MESH

NX, NZ, NY = 4, 8, 4
TILES = 64
RAYS = 256
LANES = 128
GROUP = 4
STEPS = TILES // GROUP
ROWS = 72
USED = 66
CHUNKS = 8
FORWARD = 3
TOP = 32700.0


def softplus(x):
    return jnp.maximum(x, 0.0) + jnp.log1p(jnp.exp(-jnp.abs(x)))


def put(ref, color, light):
    ref[0:32, :] = color[:, :LANES]
    ref[32:64, :] = color[:, LANES:]
    ref[64:65, :] = light[:, :LANES]
    ref[65:66, :] = light[:, LANES:]


def get(ref):
    return ref[0:32, :], ref[32:64, :], ref[64:65, :], ref[65:66, :]


def ordered(pieces):
    left, right, tleft, tright = pieces[0]
    for a, b, ta, tb in pieces[1:]:
        left = left + tleft * a
        right = right + tright * b
        tleft = tleft * ta
        tright = tright * tb
    return left, right, tleft, tright


def put4(ref, piece):
    ref[0:32, :] = piece[0]
    ref[32:64, :] = piece[1]
    ref[64:65, :] = piece[2]
    ref[65:66, :] = piece[3]


def kernel(
    bricks, index_hbm, interp, step_hbm, count_hbm, w1_hbm, w2_hbm, wo_hbm,
    color_out, light_out,
    table_bf, index, wv, step, count, w1, w2, wo, w2t,
    stage, table, h1a, h1b, h2a, h2b,
    mine, csend, crecv, zsend, zrecv, zmsend, zmrecv, xsend, xrecv,
    in_sem, wv_sem, ysend_sem, yrecv_sem, cs_sem, cr_sem, zs_sem, zr_sem, xs_sem, xr_sem,
):
    region = lax.axis_index("region")
    y = lax.axis_index("ray")
    core = lax.rem(region, 2)
    z = lax.rem(region // 2, NZ)
    x = region // (2 * NZ)

    def at(px, pz, pc):
        return {"region": px * (2 * NZ) + pz * 2 + pc}

    barrier = pltpu.get_barrier_semaphore()

    def hello(device):
        pl.semaphore_signal(barrier, inc=1, device_id=device, device_id_type=MESH)

    for d in range(1, NY):
        hello({"ray": lax.rem(y + d, NY)})
    hello(at(x, z, 1 - core))
    for d in range(1, NZ):
        hello(at(x, lax.rem(z + d, NZ), core))
    for d in range(1, NX):
        hello(at(lax.rem(x + d, NX), z, core))
    small = [
        pltpu.make_async_copy(src, dst, in_sem.at[i])
        for i, (src, dst) in enumerate(
            [
                (w1_hbm, w1), (w2_hbm, w2), (wo_hbm, wo), (index_hbm.at[0], index),
                (step_hbm.at[0], step), (count_hbm, count),
                (bricks.at[0], table_bf.at[pl.ds(y * 128, 128)]),
            ]
        )
    ]
    for copy in small:
        copy.start()

    def wv_copy(c):
        n = TILES // CHUNKS
        return pltpu.make_async_copy(interp.at[0, pl.ds(c * n, n)], wv.at[pl.ds(c * n, n)], wv_sem.at[c])

    for c in range(CHUNKS):
        wv_copy(c).start()

    pl.semaphore_wait(barrier, (NY - 1) + 1 + (NZ - 1) + (NX - 1))

    def half_of(owner, h):
        return table_bf.at[pl.ds(lax.rem(owner + NY, NY) * 128 + h * 64, 64)]

    def y_copy(n):
        owner, h, to = ((y, 0, 1), (y, 1, 3), (y, 1, 1), (y, 0, 3), (y - 1, 0, 1), (y + 1, 1, 3))[n]
        return pltpu.make_async_remote_copy(
            src_ref=half_of(owner, h) if n >= 4 else bricks.at[0, pl.ds(h * 64, 64)],
            dst_ref=half_of(owner, h),
            send_sem=ysend_sem.at[n],
            recv_sem=yrecv_sem.at[n],
            device_id={"ray": lax.rem(y + to, NY)},
            device_id_type=MESH,
        )

    for n in range(4):
        y_copy(n).start()

    for copy in small:
        copy.wait()
    w2t[...] = w2[...].astype(F32).T.astype(BF)

    for c in range(CHUNKS):
        if c == FORWARD:
            for n in range(2):
                y_copy(n).wait_recv()
                y_copy(4 + n).start()
        wv_copy(c).wait()

        @pl.loop(0, TILES // CHUNKS)
        def _(i):
            t = c * (TILES // CHUNKS) + i
            b = lax.rem(i, 2)
            stage[b] = wv[t].astype(F32)
            wv[t, 0:RAYS] = stage[b, pl.ds(0, RAYS, stride=2), :].astype(BF)
            wv[t, RAYS : 2 * RAYS] = stage[b, pl.ds(1, RAYS, stride=2), :].astype(BF)

    for n in range(2, 6):
        y_copy(n).wait_recv()

    half = w1[...]
    none = jnp.zeros_like(half)
    wide = [jnp.concatenate([half, none], 0), jnp.concatenate([none, half], 0)]
    for v in range(8):
        cols = (v // 2) * LANES
        got = jnp.dot(table_bf[:, cols : cols + LANES], wide[v % 2], preferred_element_type=F32)
        flat = table.reshape(2, 4096, LANES)
        flat[0, pl.ds(v, 512, stride=8), :] = got[:, :LANES]
        flat[1, pl.ds(v, 512, stride=8), :] = got[:, LANES:]

    def offsets(i):
        j = lax.rem(i, 4)
        return 4 + j, 3 - j

    def column(k):
        return lax.rem(x + 1 + k, NX)

    def tile(i, u):
        off = offsets(i)[u % 2]
        c = core if u < 2 else 1 - core
        return column(i // 4) * (2 * NZ) + lax.rem(z + off, NZ) * 2 + c

    def layer1(i, h1):
        for u in range(GROUP):
            t = tile(i, u)
            ids = [index[j, t] for j in range(16)]
            g = [jnp.concatenate([table[h, b] for b in ids], 0).T for h in range(2)]
            g = jnp.concatenate(g, 0).astype(BF)
            r = lax.dot_general(g, wv[t], (((1,), (1,)), ((), ())), preferred_element_type=F32)
            h1[u * 256 : (u + 1) * 256] = jnp.maximum(r.astype(BF), 0)

    def layer2(h1, h2):
        for u in range(GROUP):
            r = jnp.dot(w2t[...], h1[u * 256 : (u + 1) * 256], preferred_element_type=F32)
            h2[u * 256 : (u + 1) * 256] = jnp.maximum(r.astype(BF), 0)

    def layer3(i, h2):
        for u in range(GROUP):
            t = tile(i, u)
            o = jnp.dot(wo[...], h2[u * 256 : (u + 1) * 256], preferred_element_type=F32)
            lanes = pl.ds(pl.multiple_of(t * RAYS, RAYS), RAYS)
            n = count[0:1, lanes]
            tau0 = softplus(o[32:33, :RAYS]) * step[0:1, lanes] * jnp.where(n > 0, 1.0, 0.0)
            tau1 = softplus(o[32:33, RAYS:]) * step[1:2, lanes] * jnp.where(n > 1, 1.0, 0.0)
            a0 = jnp.exp(-tau0)
            a1 = jnp.exp(-tau1)
            color = o[0:32, :RAYS] * (1.0 - a0) + o[0:32, RAYS:] * (a0 * (1.0 - a1))
            put((mine if u < 2 else csend).at[i, u % 2], color, a0 * a1)

    def c_copy(g):
        return pltpu.make_async_remote_copy(
            src_ref=csend.at[g],
            dst_ref=crecv.at[g],
            send_sem=cs_sem.at[g],
            recv_sem=cr_sem.at[g],
            device_id=at(x, z, 1 - core),
            device_id_type=MESH,
        )

    def z_copies(k, off):
        to = at(x, lax.rem(z + off, NZ), core)
        return [
            pltpu.make_async_remote_copy(
                src_ref=src.at[k, off, pl.ds(0, n)],
                dst_ref=dst.at[k, z, pl.ds(0, n)],
                send_sem=zs_sem.at[h, k, off],
                recv_sem=zr_sem.at[h, k, z],
                device_id=to,
                device_id_type=MESH,
            )
            for h, (src, dst, n) in enumerate([(zsend, zrecv, 64), (zmsend, zmrecv, 4)])
        ]

    def z_wait(k, src):
        for h, (ref, n) in enumerate([(zrecv, 64), (zmrecv, 4)]):
            got = ref.at[k, src, pl.ds(0, n)]
            pltpu.make_async_copy(got, got, zr_sem.at[h, k, src]).wait()

    def code(colors, lights, piece):
        for h in range(2):
            most = jnp.max(jnp.abs(piece[h]), axis=0, keepdims=True)
            colors[32 * h : 32 * h + 32, :] = (
                (piece[h] * (TOP / jnp.maximum(most, 1e-30))).astype(jnp.int32).astype(jnp.int16)
            )
            lights[h : h + 1, :] = piece[2 + h]
            lights[2 + h : 3 + h, :] = jnp.maximum(most, 1e-30) * (1.0 / TOP)

    def decode(colors, lights):
        halves = [
            colors[32 * h : 32 * h + 32, :].astype(jnp.int32).astype(F32) * lights[2 + h : 3 + h, :]
            for h in range(2)
        ]
        return halves[0], halves[1], lights[0:1, :], lights[1:2, :]

    def x_copy(k):
        return pltpu.make_async_remote_copy(
            src_ref=xsend.at[k, pl.ds(0, USED)],
            dst_ref=xrecv.at[x, pl.ds(0, USED)],
            send_sem=xs_sem.at[k],
            recv_sem=xr_sem.at[x],
            device_id=at(column(k), z, core),
            device_id_type=MESH,
        )

    def merge_cores(g):
        c_copy(g).wait_recv()
        front = core == 0
        k = g // 4
        off = offsets(g)
        for u in range(2):
            a, b = get(mine.at[g, u]), get(crecv.at[g, u])
            near = [jnp.where(front, p, q) for p, q in zip(a, b)]
            far = [jnp.where(front, q, p) for p, q in zip(a, b)]
            piece = ordered([near, far])
            if u == 0:
                code(zsend.at[k, off[0]], zmsend.at[k, off[0]], piece)
                for copy in z_copies(k, off[0]):
                    copy.start()
            else:
                own = lax.rem(g, 4) == 3

                @pl.when(own)
                def _():
                    code(zrecv.at[k, z], zmrecv.at[k, z], piece)

                @pl.when(jnp.logical_not(own))
                def _():
                    code(zsend.at[k, off[1]], zmsend.at[k, off[1]], piece)
                    for copy in z_copies(k, off[1]):
                        copy.start()

    def merge_z(k):
        @pl.loop(1, NZ)
        def _(d):
            z_wait(k, lax.rem(z + d, NZ))

        return ordered([decode(zrecv.at[k, s], zmrecv.at[k, s]) for s in range(NZ)])

    def hand_on(k):
        put4(xsend.at[k], merge_z(k))
        x_copy(k).start()

    def finish(i, h2):
        layer3(i, h2)
        c_copy(i).start()

    def work(i, now, before):
        layer3(i - 2, now[1])
        layer2(before[0], before[1])
        layer1(i, now[0])
        c_copy(i - 2).start()

        @pl.when(i >= 4)
        def _():
            merge_cores(i - 4)

        @pl.when(jnp.logical_and(i >= 11, lax.rem(i, 4) == 3))
        def _():
            hand_on((i - 11) // 4)

    even, odd = (h1a, h2a), (h1b, h2b)
    layer1(0, h1a)
    layer2(h1a, h2a)
    layer1(1, h1b)

    @pl.loop(1, STEPS // 2)
    def _(n):
        work(2 * n, even, odd)
        work(2 * n + 1, odd, even)

    layer3(STEPS - 2, h2a)
    layer2(h1b, h2b)
    c_copy(STEPS - 2).start()
    layer3(STEPS - 1, h2b)
    c_copy(STEPS - 1).start()

    @pl.loop(STEPS - 4, STEPS)
    def _(g):
        merge_cores(g)

    hand_on(2)
    put4(xrecv.at[x], merge_z(3))
    for d in range(1, NX):
        src = lax.rem(x + d, NX)
        pltpu.make_async_copy(xrecv.at[src, pl.ds(0, USED)], xrecv.at[src, pl.ds(0, USED)], xr_sem.at[src]).wait()
    left, right, tleft, tright = ordered([get(xrecv.at[s]) for s in range(NX)])
    color_out[:, :LANES] = left
    color_out[:, LANES:] = right
    light_out[:, :LANES] = tleft
    light_out[:, LANES:] = tright

    for n in range(6):
        y_copy(n).wait_send()

    @pl.loop(0, STEPS)
    def _(g):
        c_copy(g).wait_send()
        for copy in z_copies(g // 4, offsets(g)[0]):
            copy.wait_send()

        @pl.when(lax.rem(g, 4) < 3)
        def _():
            for copy in z_copies(g // 4, offsets(g)[1]):
                copy.wait_send()

    for k in range(3):
        x_copy(k).wait_send()


def shards(bricks, pair_index, interp_weight, step_len, sample_count, w_first, w_second, w_out):
    part = functools.partial(pltpu.VMEM, dtype=F32)
    dma = pltpu.SemaphoreType.DMA
    color, light = pl.pallas_call(
        kernel,
        out_shape=(jax.ShapeDtypeStruct((32, RAYS), F32), jax.ShapeDtypeStruct((1, RAYS), F32)),
        in_specs=[pl.BlockSpec(memory_space=pltpu.HBM)] * 8,
        out_specs=[pl.BlockSpec(memory_space=pltpu.VMEM)] * 2,
        scratch_shapes=[
            pltpu.VMEM((512, 512), BF),
            pltpu.SMEM((16, 64), jnp.int32),
            pltpu.VMEM((TILES, 2 * RAYS, LANES), BF),
            pltpu.VMEM((2, TILES * RAYS), F32),
            pltpu.VMEM((1, TILES * RAYS), jnp.int32),
            pltpu.VMEM((64, 256), BF),
            pltpu.VMEM((256, 256), BF),
            pltpu.VMEM((33, 256), BF),
            pltpu.VMEM((256, 256), BF),
            pltpu.VMEM((2, 2 * RAYS, LANES), F32),
            pltpu.VMEM((2, 512, 8, LANES), F32),
        ]
        + [pltpu.VMEM((GROUP * 256, 512), BF)] * 4
        + [part((STEPS, 2, ROWS, LANES))] * 3
        + [pltpu.VMEM((NX, NZ, 64, LANES), jnp.int16)] * 2
        + [part((NX, NZ, 8, LANES))] * 2
        + [part((NX, ROWS, LANES))] * 2
        + [dma((7,)), dma((CHUNKS,)), dma((6,)), dma((6,)), dma((STEPS,)), dma((STEPS,))]
        + [dma((2, NX, NZ)), dma((2, NX, NZ)), dma((NX,)), dma((NX,))],
        compiler_params=pltpu.CompilerParams(
            collective_id=0, has_side_effects=True, vmem_limit_bytes=62 * 2**20
        ),
        name="render",
    )(
        bricks,
        jnp.swapaxes(pair_index, 1, 2),
        interp_weight,
        step_len,
        sample_count,
        w_first,
        w_second,
        w_out.T,
    )
    return color, light.reshape(RAYS)


def solution(mesh):
    return jax.shard_map(
        shards,
        mesh=mesh,
        in_specs=(
            P("region", "ray", None),
            P("region", "ray", None),
            P("region", "ray", None, None),
            P("region", None, "ray"),
            P("region", "ray"),
            P(),
            P(),
            P(),
        ),
        out_specs=(P(None, ("ray", "region")), P(("ray", "region"))),
        check_vma=False,
    )
```

```python
import functools

import jax
import jax.numpy as jnp
from jax import lax
from jax.experimental import pallas as pl
from jax.experimental.pallas import tpu as pltpu
from jax.sharding import PartitionSpec as P

BF = jnp.bfloat16
F32 = jnp.float32
MESH = pl.DeviceIdType.MESH

NX, NZ, NY = 4, 8, 4
TILES = 64
RAYS = 256
LANES = 128
GROUP = 4
PAIRS = TILES // 4
LEAD = 4
STEPS = TILES // GROUP
ROWS = 72
USED = 66
CHUNKS = 8
FORWARD = 3
FINE = 2.0**20
TOP = 32700.0


def softplus(x):
    return jnp.maximum(x, 0.0) + jnp.log1p(jnp.exp(-jnp.abs(x)))


def put(ref, color, light):
    ref[0:32, :] = color[:, :LANES]
    ref[32:64, :] = color[:, LANES:]
    ref[64:65, :] = light[:, :LANES]
    ref[65:66, :] = light[:, LANES:]


def get(ref):
    return ref[0:32, :], ref[32:64, :], ref[64:65, :], ref[65:66, :]


def ordered(pieces):
    left, right, tleft, tright = pieces[0]
    for a, b, ta, tb in pieces[1:]:
        left = left + tleft * a
        right = right + tright * b
        tleft = tleft * ta
        tright = tright * tb
    return left, right, tleft, tright


def put4(ref, piece):
    ref[0:32, :] = piece[0]
    ref[32:64, :] = piece[1]
    ref[64:65, :] = piece[2]
    ref[65:66, :] = piece[3]


def kernel(
    bricks, index_hbm, interp, step_hbm, count_hbm, w1_hbm, w2_hbm, wo_hbm,
    color_out, light_out,
    table_bf, index, wv, step, count, w1, w2, wo, w2t,
    stage, table, h1a, h1b, h2a, h2b,
    csend, crecv, zsend, zrecv, xsend, xrecv,
    in_sem, wv_sem, ysend_sem, yrecv_sem, cs_sem, cr_sem, zs_sem, zr_sem, xs_sem, xr_sem,
):
    region = lax.axis_index("region")
    y = lax.axis_index("ray")
    core = lax.rem(region, 2)
    z = lax.rem(region // 2, NZ)
    x = region // (2 * NZ)

    def at(px, pz, pc):
        return {"region": px * (2 * NZ) + pz * 2 + pc}

    barrier = pltpu.get_barrier_semaphore()

    def hello(device):
        pl.semaphore_signal(barrier, inc=1, device_id=device, device_id_type=MESH)

    for d in range(1, NY):
        hello({"ray": lax.rem(y + d, NY)})
    hello(at(x, z, 1 - core))
    for d in range(1, NZ):
        hello(at(x, lax.rem(z + d, NZ), core))
    for d in range(1, NX):
        hello(at(lax.rem(x + d, NX), z, core))
    small = [
        pltpu.make_async_copy(src, dst, in_sem.at[i])
        for i, (src, dst) in enumerate(
            [
                (w1_hbm, w1), (w2_hbm, w2), (wo_hbm, wo), (index_hbm.at[0], index),
                (step_hbm.at[0], step), (count_hbm, count),
                (bricks.at[0], table_bf.at[pl.ds(y * 128, 128)]),
            ]
        )
    ]
    for copy in small:
        copy.start()

    def wv_copy(c):
        n = TILES // CHUNKS
        return pltpu.make_async_copy(interp.at[0, pl.ds(c * n, n)], wv.at[pl.ds(c * n, n)], wv_sem.at[c])

    for c in range(CHUNKS):
        wv_copy(c).start()

    pl.semaphore_wait(barrier, (NY - 1) + 1 + (NZ - 1) + (NX - 1))

    def half_of(owner, h):
        return table_bf.at[pl.ds(lax.rem(owner + NY, NY) * 128 + h * 64, 64)]

    def y_copy(n):
        owner, h, to = ((y, 0, 1), (y, 1, 3), (y, 1, 1), (y, 0, 3), (y - 1, 0, 1), (y + 1, 1, 3))[n]
        return pltpu.make_async_remote_copy(
            src_ref=half_of(owner, h) if n >= 4 else bricks.at[0, pl.ds(h * 64, 64)],
            dst_ref=half_of(owner, h),
            send_sem=ysend_sem,
            recv_sem=yrecv_sem.at[n],
            device_id={"ray": lax.rem(y + to, NY)},
            device_id_type=MESH,
        )

    for n in range(4):
        y_copy(n).start()

    for copy in small:
        copy.wait()
    w2t[...] = w2[...].astype(F32).T.astype(BF)

    for c in range(CHUNKS):
        if c == FORWARD:
            for n in range(2):
                y_copy(n).wait_recv()
                y_copy(4 + n).start()
        wv_copy(c).wait()

        @pl.loop(0, TILES // CHUNKS)
        def _(i):
            t = c * (TILES // CHUNKS) + i
            b = lax.rem(i, 2)
            stage[b] = wv[t].astype(F32)
            wv[t, 0:RAYS] = stage[b, pl.ds(0, RAYS, stride=2), :].astype(BF)
            wv[t, RAYS : 2 * RAYS] = stage[b, pl.ds(1, RAYS, stride=2), :].astype(BF)

    for n in range(2, 6):
        y_copy(n).wait_recv()

    half = w1[...]
    none = jnp.zeros_like(half)
    wide = [jnp.concatenate([half, none], 0), jnp.concatenate([none, half], 0)]
    for v in range(8):
        cols = (v // 2) * LANES
        got = jnp.dot(table_bf[:, cols : cols + LANES], wide[v % 2], preferred_element_type=F32)
        flat = table.reshape(2, 4096, LANES)
        flat[0, pl.ds(v, 512, stride=8), :] = got[:, :LANES]
        flat[1, pl.ds(v, 512, stride=8), :] = got[:, LANES:]

    def offsets(p):
        j = lax.rem(p, 4)
        return 4 + j, 3 - j

    def column(k):
        return lax.rem(x + 1 + k, NX)

    def tile(p, u, c):
        return column(p // 4) * (2 * NZ) + lax.rem(z + offsets(p)[u], NZ) * 2 + c

    def tiles(i):
        first, last = i < LEAD // 2, i >= STEPS - LEAD // 2
        a = jnp.where(first, 2 * i, jnp.where(last, 2 * i - PAIRS, i + LEAD // 2))
        b = jnp.where(first, 2 * i + 1, jnp.where(last, 2 * i - PAIRS + 1, i - LEAD // 2))
        ca = jnp.where(last, core, 1 - core)
        cb = jnp.where(first, 1 - core, core)
        return [tile(a, 0, ca), tile(a, 1, ca), tile(b, 0, cb), tile(b, 1, cb)]

    def layer1(i, h1):
        for u, t in enumerate(tiles(i)):
            ids = [index[j, t] for j in range(16)]
            g = [jnp.concatenate([table[h, b] for b in ids], 0).T for h in range(2)]
            g = jnp.concatenate(g, 0).astype(BF)
            r = lax.dot_general(g, wv[t], (((1,), (1,)), ((), ())), preferred_element_type=F32)
            h1[u * 256 : (u + 1) * 256] = jnp.maximum(r.astype(BF), 0)

    def layer2(h1, h2):
        for u in range(GROUP):
            r = jnp.dot(w2t[...], h1[u * 256 : (u + 1) * 256], preferred_element_type=F32)
            h2[u * 256 : (u + 1) * 256] = jnp.maximum(r.astype(BF), 0)

    def shade(h2, u, t):
        o = jnp.dot(wo[...], h2[u * 256 : (u + 1) * 256], preferred_element_type=F32)
        lanes = pl.ds(pl.multiple_of(t * RAYS, RAYS), RAYS)
        n = count[0:1, lanes]
        tau0 = softplus(o[32:33, :RAYS]) * step[0:1, lanes] * jnp.where(n > 0, 1.0, 0.0)
        tau1 = softplus(o[32:33, RAYS:]) * step[1:2, lanes] * jnp.where(n > 1, 1.0, 0.0)
        a0 = jnp.exp(-tau0)
        a1 = jnp.exp(-tau1)
        color = o[0:32, :RAYS] * (1.0 - a0) + o[0:32, RAYS:] * (a0 * (1.0 - a1))
        return color, a0 * a1

    def shade_other(p, h2, u):
        for v in range(2):
            put(csend.at[p, v], *shade(h2, u + v, tile(p, v, 1 - core)))

    def shade_own(p, h2, u):
        front = core == 0
        for v in range(2):
            color, light = shade(h2, u + v, tile(p, v, core))
            left, right, tleft, tright = get(crecv.at[p, v])
            piece = []
            for a, ta, b, tb in (
                (color[:, :LANES], light[:, :LANES], left, tleft),
                (color[:, LANES:], light[:, LANES:], right, tright),
            ):
                piece.append(a * jnp.where(front, 1.0, tb) + b * jnp.where(front, ta, 1.0))
                piece.append(ta * tb)
            off = offsets(p)[v]
            code(zsend.at[p // 4, off], piece[0::2] + piece[1::2])

    def c_copy(n):
        return pltpu.make_async_remote_copy(
            src_ref=csend.at[pl.ds(2 * n, 2)],
            dst_ref=crecv.at[pl.ds(2 * n, 2)],
            send_sem=cs_sem,
            recv_sem=cr_sem.at[n],
            device_id=at(x, z, 1 - core),
            device_id_type=MESH,
        )

    def wait_for(ref, sem):
        pltpu.make_async_copy(ref, ref, sem).wait()

    def z_copy(k, off):
        return pltpu.make_async_remote_copy(
            src_ref=zsend.at[k, off],
            dst_ref=zrecv.at[k, z],
            send_sem=zs_sem,
            recv_sem=zr_sem.at[k],
            device_id=at(x, lax.rem(z + off, NZ), core),
            device_id_type=MESH,
        )

    def code(ref, piece):
        row = lax.broadcasted_iota(jnp.int32, (16, LANES), 0)
        kind = jnp.bitwise_and(row, 3)
        top = []
        for h in range(2):
            most = jnp.maximum(jnp.max(jnp.abs(piece[h]), axis=0, keepdims=True), 1e-30)
            ref[32 * h : 32 * h + 32, :] = (piece[h] * (TOP / most)).astype(jnp.int32).astype(jnp.int16)
            top.append(most * (1.0 / TOP))
        value = jnp.where(
            kind < 2,
            jnp.where(kind == 0, piece[2], piece[3]),
            jnp.where(kind == 2, top[0], top[1]),
        )
        fixed = (jnp.log(jnp.maximum(value, 1e-37)) * FINE).astype(jnp.int32)
        parts = jnp.where(row < 4, jnp.right_shift(fixed, 15), jnp.bitwise_and(fixed, 32767))
        ref[64:80, :] = jnp.where(row < 8, parts, 0).astype(jnp.int16)

    def decode(ref):
        parts = ref[64:80, :].astype(jnp.int32)
        value = jnp.exp(parts[0:4].astype(F32) * (32768.0 / FINE) + parts[4:8].astype(F32) * (1.0 / FINE))
        halves = [
            ref[32 * h : 32 * h + 32, :].astype(jnp.int32).astype(F32) * value[2 + h : 3 + h] for h in range(2)
        ]
        return halves[0], halves[1], value[0:1], value[1:2]

    def x_copy(k):
        return pltpu.make_async_remote_copy(
            src_ref=xsend.at[k, pl.ds(0, USED)],
            dst_ref=xrecv.at[x, pl.ds(0, USED)],
            send_sem=xs_sem,
            recv_sem=xr_sem,
            device_id=at(column(k), z, core),
            device_id_type=MESH,
        )

    def send_own(p):
        k, off = p // 4, offsets(p)
        z_copy(k, off[0]).start()
        own = lax.rem(p, 4) == 3

        @pl.when(own)
        def _():
            zrecv[k, z] = zsend[k, 0]

        @pl.when(jnp.logical_not(own))
        def _():
            z_copy(k, off[1]).start()

    def merge_z(k):
        wait_for(zrecv.at[k, pl.ds(0, NZ - 1)], zr_sem.at[k])
        return ordered([decode(zrecv.at[k, s]) for s in range(NZ)])

    def hand_on(k):
        put4(xsend.at[k], merge_z(k))
        x_copy(k).start()

    def compute(i, now, before):
        layer2(before[0], before[1])
        layer1(i, now[0])

    def work(i, now, before):
        shade_other(i, now[1], 0)
        shade_own(i - 4, now[1], 2)
        compute(i, now, before)
        send_own(i - 4)

    even, odd = (h1a, h2a), (h1b, h2b)
    layer1(0, h1a)
    layer2(h1a, h2a)
    layer1(1, h1b)
    for i in range(2, 4):
        now, before = (even, odd) if i % 2 == 0 else (odd, even)
        first = 2 * (i - 2)
        for n in range(2):
            shade_other(first + n, now[1], 2 * n)
        compute(i, now, before)
        c_copy(i - 2).start()

    @pl.loop(2, STEPS // 2)
    def _(n):
        c_copy(n - 2).wait_recv()
        work(2 * n, even, odd)

        work(2 * n + 1, odd, even)
        c_copy(n).start()

    for i in range(2):
        now = even if i == 0 else odd
        first = PAIRS - LEAD + 2 * i
        c_copy(first // 2).wait_recv()
        for n in range(2):
            shade_own(first + n, now[1], 2 * n)
        if i == 0:
            layer2(h1b, h2b)
        for n in range(2):
            send_own(first + n)
    for k in range(3):
        hand_on(k)
    put4(xrecv.at[x], merge_z(3))
    wait_for(xrecv.at[pl.ds(0, NX - 1), pl.ds(0, USED)], xr_sem)
    left, right, tleft, tright = ordered([get(xrecv.at[s]) for s in range(NX)])
    color_out[:, :LANES] = left
    color_out[:, LANES:] = right
    light_out[:, :LANES] = tleft
    light_out[:, LANES:] = tright

    wait_for(table_bf.at[pl.ds(0, 384)], ysend_sem)
    wait_for(csend, cs_sem)
    wait_for(zsend.at[:, pl.ds(1, NZ - 1)], zs_sem)
    wait_for(xsend.at[pl.ds(0, NX - 1), pl.ds(0, USED)], xs_sem)


def shards(bricks, pair_index, interp_weight, step_len, sample_count, w_first, w_second, w_out):
    part = functools.partial(pltpu.VMEM, dtype=F32)
    dma = pltpu.SemaphoreType.DMA
    color, light = pl.pallas_call(
        kernel,
        out_shape=(jax.ShapeDtypeStruct((32, RAYS), F32), jax.ShapeDtypeStruct((1, RAYS), F32)),
        in_specs=[pl.BlockSpec(memory_space=pltpu.HBM)] * 8,
        out_specs=[pl.BlockSpec(memory_space=pltpu.VMEM)] * 2,
        scratch_shapes=[
            pltpu.VMEM((512, 512), BF),
            pltpu.SMEM((16, 64), jnp.int32),
            pltpu.VMEM((TILES, 2 * RAYS, LANES), BF),
            pltpu.VMEM((2, TILES * RAYS), F32),
            pltpu.VMEM((1, TILES * RAYS), jnp.int32),
            pltpu.VMEM((64, 256), BF),
            pltpu.VMEM((256, 256), BF),
            pltpu.VMEM((33, 256), BF),
            pltpu.VMEM((256, 256), BF),
            pltpu.VMEM((2, 2 * RAYS, LANES), F32),
            pltpu.VMEM((2, 512, 8, LANES), F32),
        ]
        + [pltpu.VMEM((GROUP * 256, 512), BF)] * 4
        + [part((PAIRS, 2, ROWS, LANES))] * 2
        + [pltpu.VMEM((NX, NZ, 80, LANES), jnp.int16)] * 2
        + [part((NX, ROWS, LANES))] * 2
        + [dma((7,)), dma((CHUNKS,)), dma, dma((6,)), dma, dma((PAIRS // 2,))]
        + [dma, dma((NX,)), dma, dma],
        compiler_params=pltpu.CompilerParams(
            collective_id=0, has_side_effects=True, vmem_limit_bytes=62 * 2**20
        ),
        name="render",
    )(
        bricks,
        jnp.swapaxes(pair_index, 1, 2),
        interp_weight,
        step_len,
        sample_count,
        w_first,
        w_second,
        w_out.T,
    )
    return color, light.reshape(RAYS)


def solution(mesh):
    return jax.shard_map(
        shards,
        mesh=mesh,
        in_specs=(
            P("region", "ray", None),
            P("region", "ray", None),
            P("region", "ray", None, None),
            P("region", None, "ray"),
            P("region", "ray"),
            P(),
            P(),
            P(),
        ),
        out_specs=(P(None, ("ray", "region")), P(("ray", "region"))),
        check_vma=False,
    )
```

```python
import functools

import jax
import jax.numpy as jnp
from jax import lax
from jax.experimental import pallas as pl
from jax.experimental.pallas import tpu as pltpu
from jax.sharding import PartitionSpec as P

BF = jnp.bfloat16
F32 = jnp.float32
MESH = pl.DeviceIdType.MESH

NX, NZ, NY = 4, 8, 4
TILES = 64
RAYS = 256
LANES = 128
GROUP = 4
PAIRS = TILES // 4
LEAD = 4
STEPS = TILES // GROUP
ROWS = 72
USED = 66
CHUNKS = 8
FORWARD = (2, 3)
FINE = 2.0**20
TOP = 32700.0


def softplus(x):
    return jnp.maximum(x, 0.0) + jnp.log1p(jnp.exp(-jnp.abs(x)))


def put(ref, color, light):
    ref[0:32, :] = color[:, :LANES]
    ref[32:64, :] = color[:, LANES:]
    ref[64:65, :] = light[:, :LANES]
    ref[65:66, :] = light[:, LANES:]


def get(ref):
    return ref[0:32, :], ref[32:64, :], ref[64:65, :], ref[65:66, :]


def ordered(pieces):
    left, right, tleft, tright = pieces[0]
    for a, b, ta, tb in pieces[1:]:
        left = left + tleft * a
        right = right + tright * b
        tleft = tleft * ta
        tright = tright * tb
    return left, right, tleft, tright


def put4(ref, piece):
    ref[0:32, :] = piece[0]
    ref[32:64, :] = piece[1]
    ref[64:65, :] = piece[2]
    ref[65:66, :] = piece[3]


def kernel(
    bricks, index_hbm, interp, step_hbm, count_hbm, w1_hbm, w2_hbm, wo_hbm,
    color_out, light_out,
    table_bf, index, wv, step, count, w1, w2, wo, w2t,
    stage, table, h1a, h1b, h2a, h2b,
    csend, crecv, zsend, zrecv, xsend, xrecv,
    in_sem, wv_sem, ysend_sem, yrecv_sem, cs_sem, cr_sem, zs_sem, zr_sem, xs_sem, xr_sem,
):
    region = lax.axis_index("region")
    y = lax.axis_index("ray")
    core = lax.rem(region, 2)
    z = lax.rem(region // 2, NZ)
    x = region // (2 * NZ)

    def at(px, pz, pc):
        return {"region": px * (2 * NZ) + pz * 2 + pc}

    barrier = pltpu.get_barrier_semaphore()

    def hello(device):
        pl.semaphore_signal(barrier, inc=1, device_id=device, device_id_type=MESH)

    for d in range(1, NY):
        hello({"ray": lax.rem(y + d, NY)})
    hello(at(x, z, 1 - core))
    for d in range(1, NZ):
        hello(at(x, lax.rem(z + d, NZ), core))
    for d in range(1, NX):
        hello(at(lax.rem(x + d, NX), z, core))
    small = [
        pltpu.make_async_copy(src, dst, in_sem.at[i])
        for i, (src, dst) in enumerate(
            [
                (w1_hbm, w1), (w2_hbm, w2), (wo_hbm, wo), (index_hbm.at[0], index),
                (step_hbm.at[0], step), (count_hbm, count),
                (bricks.at[0], table_bf.at[pl.ds(y * 128, 128)]),
            ]
        )
    ]
    def wv_copy(c):
        n = TILES // CHUNKS
        return pltpu.make_async_copy(interp.at[0, pl.ds(c * n, n)], wv.at[pl.ds(c * n, n)], wv_sem.at[c])

    for c in range(CHUNKS):
        wv_copy(c).start()

    pl.semaphore_wait(barrier, (NY - 1) + 1 + (NZ - 1) + (NX - 1))

    def y_rows(owner, first):
        return table_bf.at[pl.ds(lax.rem(owner + NY, NY) * 128 + first, 32)]

    y_plan = [(y, 0, 1), (y, 64, 3), (y, 32, 1), (y, 96, 3), (y, 64, 1), (y, 0, 3), (y, 96, 1), (y, 32, 3)]
    y_plan += [(y - 1, 0, 1), (y + 1, 64, 3), (y - 1, 32, 1), (y + 1, 96, 3)]

    def y_copy(n):
        owner, first, to = y_plan[n]
        return pltpu.make_async_remote_copy(
            src_ref=y_rows(owner, first) if n >= 8 else bricks.at[0, pl.ds(first, 32)],
            dst_ref=y_rows(owner, first),
            send_sem=ysend_sem,
            recv_sem=yrecv_sem.at[n],
            device_id={"ray": lax.rem(y + to, NY)},
            device_id_type=MESH,
        )

    for n in range(8):
        y_copy(n).start()

    for copy in small:
        copy.start()

    for copy in small:
        copy.wait()
    w2t[...] = w2[...].astype(F32).T.astype(BF)

    for c in range(CHUNKS):
        if c in FORWARD:
            for n in range(2):
                n += 2 * FORWARD.index(c)
                y_copy(n).wait_recv()
                y_copy(8 + n).start()
        wv_copy(c).wait()

        @pl.loop(0, TILES // CHUNKS)
        def _(i):
            t = c * (TILES // CHUNKS) + i
            b = lax.rem(i, 2)
            stage[b] = wv[t].astype(F32)
            wv[t, 0:RAYS] = stage[b, pl.ds(0, RAYS, stride=2), :].astype(BF)
            wv[t, RAYS : 2 * RAYS] = stage[b, pl.ds(1, RAYS, stride=2), :].astype(BF)

    half = w1[...]
    none = jnp.zeros_like(half)
    wide = [jnp.concatenate([half, none], 0), jnp.concatenate([none, half], 0)]
    flat = table.reshape(2, 4096, LANES)

    def fold(owner):
        first = pl.multiple_of(lax.rem(owner + NY, NY) * 128, 128)
        for v in range(8):
            block = table_bf[pl.ds(first, 128), v // 2 * LANES : v // 2 * LANES + LANES]
            got = jnp.dot(block, wide[v % 2], preferred_element_type=F32)
            for h in range(2):
                flat[h, pl.ds(first * 8 + v, 128, stride=8), :] = got[:, h * LANES : (h + 1) * LANES]

    for owner, arrivals in ((y, ()), (y - 1, (4, 6)), (y + 1, (5, 7)), (y + 2, (8, 9, 10, 11))):
        for n in arrivals:
            y_copy(n).wait_recv()
        fold(owner)

    def offsets(p):
        j = lax.rem(p, 4)
        return 4 + j, 3 - j

    def column(k):
        return lax.rem(x + 1 + k, NX)

    def tile(p, u, c):
        return column(p // 4) * (2 * NZ) + lax.rem(z + offsets(p)[u], NZ) * 2 + c

    def tiles(i):
        first, last = i < LEAD // 2, i >= STEPS - LEAD // 2
        a = jnp.where(first, 2 * i, jnp.where(last, 2 * i - PAIRS, i + LEAD // 2))
        b = jnp.where(first, 2 * i + 1, jnp.where(last, 2 * i - PAIRS + 1, i - LEAD // 2))
        ca = jnp.where(last, core, 1 - core)
        cb = jnp.where(first, 1 - core, core)
        return [tile(a, 0, ca), tile(a, 1, ca), tile(b, 0, cb), tile(b, 1, cb)]

    def layer1(i, h1):
        for u, t in enumerate(tiles(i)):
            ids = [index[j, t] for j in range(16)]
            g = [jnp.concatenate([table[h, b] for b in ids], 0).T for h in range(2)]
            g = jnp.concatenate(g, 0).astype(BF)
            r = lax.dot_general(g, wv[t], (((1,), (1,)), ((), ())), preferred_element_type=F32)
            h1[u * 256 : (u + 1) * 256] = jnp.maximum(r.astype(BF), 0)

    def layer2(h1, h2):
        for u in range(GROUP):
            r = jnp.dot(w2t[...], h1[u * 256 : (u + 1) * 256], preferred_element_type=F32)
            h2[u * 256 : (u + 1) * 256] = jnp.maximum(r.astype(BF), 0)

    def shade(h2, u, t):
        o = jnp.dot(wo[...], h2[u * 256 : (u + 1) * 256], preferred_element_type=F32)
        lanes = pl.ds(pl.multiple_of(t * RAYS, RAYS), RAYS)
        n = count[0:1, lanes]
        tau0 = softplus(o[32:33, :RAYS]) * step[0:1, lanes] * jnp.where(n > 0, 1.0, 0.0)
        tau1 = softplus(o[32:33, RAYS:]) * step[1:2, lanes] * jnp.where(n > 1, 1.0, 0.0)
        a0 = jnp.exp(-tau0)
        a1 = jnp.exp(-tau1)
        color = o[0:32, :RAYS] * (1.0 - a0) + o[0:32, RAYS:] * (a0 * (1.0 - a1))
        return color, a0 * a1

    def shade_other(p, h2, u):
        for v in range(2):
            put(csend.at[p, v], *shade(h2, u + v, tile(p, v, 1 - core)))

    def shade_own(p, h2, u):
        front = core == 0
        for v in range(2):
            color, light = shade(h2, u + v, tile(p, v, core))
            left, right, tleft, tright = get(crecv.at[p, v])
            piece = []
            for a, ta, b, tb in (
                (color[:, :LANES], light[:, :LANES], left, tleft),
                (color[:, LANES:], light[:, LANES:], right, tright),
            ):
                piece.append(a * jnp.where(front, 1.0, tb) + b * jnp.where(front, ta, 1.0))
                piece.append(ta * tb)
            off = offsets(p)[v]
            code(zsend.at[p // 4, off], piece[0::2] + piece[1::2])

    def c_copy(n):
        return pltpu.make_async_remote_copy(
            src_ref=csend.at[pl.ds(2 * n, 2)],
            dst_ref=crecv.at[pl.ds(2 * n, 2)],
            send_sem=cs_sem,
            recv_sem=cr_sem.at[n],
            device_id=at(x, z, 1 - core),
            device_id_type=MESH,
        )

    def wait_for(ref, sem):
        pltpu.make_async_copy(ref, ref, sem).wait()

    def z_copy(k, off):
        return pltpu.make_async_remote_copy(
            src_ref=zsend.at[k, off],
            dst_ref=zrecv.at[k, z],
            send_sem=zs_sem,
            recv_sem=zr_sem.at[k],
            device_id=at(x, lax.rem(z + off, NZ), core),
            device_id_type=MESH,
        )

    def code(ref, piece):
        row = lax.broadcasted_iota(jnp.int32, (16, LANES), 0)
        kind = jnp.bitwise_and(row, 3)
        top = []
        for h in range(2):
            most = jnp.maximum(jnp.max(jnp.abs(piece[h]), axis=0, keepdims=True), 1e-30)
            ref[32 * h : 32 * h + 32, :] = (piece[h] * (TOP / most)).astype(jnp.int32).astype(jnp.int16)
            top.append(most * (1.0 / TOP))
        value = jnp.where(
            kind < 2,
            jnp.where(kind == 0, piece[2], piece[3]),
            jnp.where(kind == 2, top[0], top[1]),
        )
        fixed = (jnp.log(jnp.maximum(value, 1e-37)) * FINE).astype(jnp.int32)
        parts = jnp.where(row < 4, jnp.right_shift(fixed, 15), jnp.bitwise_and(fixed, 32767))
        ref[64:80, :] = jnp.where(row < 8, parts, 0).astype(jnp.int16)

    def decode(ref):
        parts = ref[64:80, :].astype(jnp.int32)
        value = jnp.exp(parts[0:4].astype(F32) * (32768.0 / FINE) + parts[4:8].astype(F32) * (1.0 / FINE))
        halves = [
            ref[32 * h : 32 * h + 32, :].astype(jnp.int32).astype(F32) * value[2 + h : 3 + h] for h in range(2)
        ]
        return halves[0], halves[1], value[0:1], value[1:2]

    def x_copy(k):
        return pltpu.make_async_remote_copy(
            src_ref=xsend.at[k, pl.ds(0, USED)],
            dst_ref=xrecv.at[x, pl.ds(0, USED)],
            send_sem=xs_sem,
            recv_sem=xr_sem,
            device_id=at(column(k), z, core),
            device_id_type=MESH,
        )

    def send_own(p):
        k, off = p // 4, offsets(p)
        z_copy(k, off[0]).start()
        own = lax.rem(p, 4) == 3

        @pl.when(own)
        def _():
            zrecv[k, z] = zsend[k, 0]

        @pl.when(jnp.logical_not(own))
        def _():
            z_copy(k, off[1]).start()

    def merge_z(k):
        wait_for(zrecv.at[k, pl.ds(0, NZ - 1)], zr_sem.at[k])
        return ordered([decode(zrecv.at[k, s]) for s in range(NZ)])

    def hand_on(k):
        put4(xsend.at[k], merge_z(k))
        x_copy(k).start()

    def compute(i, now, before):
        layer2(before[0], before[1])
        layer1(i, now[0])

    def work(i, now, before):
        shade_other(i, now[1], 0)
        shade_own(i - 4, now[1], 2)
        compute(i, now, before)
        send_own(i - 4)

    even, odd = (h1a, h2a), (h1b, h2b)
    layer1(0, h1a)
    layer2(h1a, h2a)
    layer1(1, h1b)
    for i in range(2, 4):
        now, before = (even, odd) if i % 2 == 0 else (odd, even)
        first = 2 * (i - 2)
        for n in range(2):
            shade_other(first + n, now[1], 2 * n)
        compute(i, now, before)
        c_copy(i - 2).start()

    @pl.loop(2, STEPS // 2)
    def _(n):
        c_copy(n - 2).wait_recv()
        work(2 * n, even, odd)

        work(2 * n + 1, odd, even)
        c_copy(n).start()

    for i in range(2):
        now = even if i == 0 else odd
        first = PAIRS - LEAD + 2 * i
        c_copy(first // 2).wait_recv()
        for n in range(2):
            shade_own(first + n, now[1], 2 * n)
        if i == 0:
            layer2(h1b, h2b)
        for n in range(2):
            send_own(first + n)
    for k in range(3):
        hand_on(k)
    put4(xrecv.at[x], merge_z(3))
    wait_for(xrecv.at[pl.ds(0, NX - 1), pl.ds(0, USED)], xr_sem)
    left, right, tleft, tright = ordered([get(xrecv.at[s]) for s in range(NX)])
    color_out[:, :LANES] = left
    color_out[:, LANES:] = right
    light_out[:, :LANES] = tleft
    light_out[:, LANES:] = tright

    wait_for(table_bf.at[pl.ds(0, 384)], ysend_sem)
    wait_for(csend, cs_sem)
    wait_for(zsend.at[:, pl.ds(1, NZ - 1)], zs_sem)
    wait_for(xsend.at[pl.ds(0, NX - 1), pl.ds(0, USED)], xs_sem)


def shards(bricks, pair_index, interp_weight, step_len, sample_count, w_first, w_second, w_out):
    part = functools.partial(pltpu.VMEM, dtype=F32)
    dma = pltpu.SemaphoreType.DMA
    color, light = pl.pallas_call(
        kernel,
        out_shape=(jax.ShapeDtypeStruct((32, RAYS), F32), jax.ShapeDtypeStruct((1, RAYS), F32)),
        in_specs=[pl.BlockSpec(memory_space=pltpu.HBM)] * 8,
        out_specs=[pl.BlockSpec(memory_space=pltpu.VMEM)] * 2,
        scratch_shapes=[
            pltpu.VMEM((512, 512), BF),
            pltpu.SMEM((16, 64), jnp.int32),
            pltpu.VMEM((TILES, 2 * RAYS, LANES), BF),
            pltpu.VMEM((2, TILES * RAYS), F32),
            pltpu.VMEM((1, TILES * RAYS), jnp.int32),
            pltpu.VMEM((64, 256), BF),
            pltpu.VMEM((256, 256), BF),
            pltpu.VMEM((33, 256), BF),
            pltpu.VMEM((256, 256), BF),
            pltpu.VMEM((2, 2 * RAYS, LANES), F32),
            pltpu.VMEM((2, 512, 8, LANES), F32),
        ]
        + [pltpu.VMEM((GROUP * 256, 512), BF)] * 4
        + [part((PAIRS, 2, ROWS, LANES))] * 2
        + [pltpu.VMEM((NX, NZ, 80, LANES), jnp.int16)] * 2
        + [part((NX, ROWS, LANES))] * 2
        + [dma((7,)), dma((CHUNKS,)), dma, dma((12,)), dma, dma((PAIRS // 2,))]
        + [dma, dma((NX,)), dma, dma],
        compiler_params=pltpu.CompilerParams(
            collective_id=0, has_side_effects=True, vmem_limit_bytes=62 * 2**20
        ),
        name="render",
    )(
        bricks,
        jnp.swapaxes(pair_index, 1, 2),
        interp_weight,
        step_len,
        sample_count,
        w_first,
        w_second,
        w_out.T,
    )
    return color, light.reshape(RAYS)


def solution(mesh):
    return jax.shard_map(
        shards,
        mesh=mesh,
        in_specs=(
            P("region", "ray", None),
            P("region", "ray", None),
            P("region", "ray", None, None),
            P("region", None, "ray"),
            P("region", "ray"),
            P(),
            P(),
            P(),
        ),
        out_specs=(P(None, ("ray", "region")), P(("ray", "region"))),
        check_vma=False,
    )
```

```python
import functools

import jax
import jax.numpy as jnp
from jax import lax
from jax.experimental import pallas as pl
from jax.experimental.pallas import tpu as pltpu
from jax.sharding import PartitionSpec as P

BF = jnp.bfloat16
F32 = jnp.float32
MESH = pl.DeviceIdType.MESH

NX, NZ, NY = 4, 8, 4
TILES = 64
RAYS = 256
LANES = 128
GROUP = 4
PAIRS = TILES // 4
LEAD = 4
STEPS = TILES // GROUP
ROWS = 72
USED = 66
CHUNKS = 8
FORWARD = (2, 3)
FINE = 2.0**20
TOP = 32700.0


def softplus(x):
    return jnp.maximum(x, 0.0) + jnp.log1p(jnp.exp(-jnp.abs(x)))


def put(ref, color, light):
    ref[0:32, :] = color[:, :LANES]
    ref[32:64, :] = color[:, LANES:]
    ref[64:65, :] = light[:, :LANES]
    ref[65:66, :] = light[:, LANES:]


def get(ref):
    return ref[0:32, :], ref[32:64, :], ref[64:65, :], ref[65:66, :]


def ordered(pieces):
    left, right, tleft, tright = pieces[0]
    for a, b, ta, tb in pieces[1:]:
        left = left + tleft * a
        right = right + tright * b
        tleft = tleft * ta
        tright = tright * tb
    return left, right, tleft, tright


def put4(ref, piece):
    ref[0:32, :] = piece[0]
    ref[32:64, :] = piece[1]
    ref[64:65, :] = piece[2]
    ref[65:66, :] = piece[3]


def kernel(
    bricks, index_hbm, interp, step_hbm, count_hbm, w1_hbm, w2_hbm, wo_hbm,
    color_out, light_out,
    table_bf, index, wv, step, count, w1, w2, wo, w2t,
    stage, table, h1a, h1b, h2a, h2b,
    csend, crecv, zsend, zrecv, xsend, xrecv,
    in_sem, wv_sem, ysend_sem, yrecv_sem, cs_sem, cr_sem, zs_sem, zr_sem, xs_sem, xr_sem,
):
    region = lax.axis_index("region")
    y = lax.axis_index("ray")
    core = lax.rem(region, 2)
    z = lax.rem(region // 2, NZ)
    x = region // (2 * NZ)

    def at(px, pz, pc):
        return {"region": px * (2 * NZ) + pz * 2 + pc}

    barrier = pltpu.get_barrier_semaphore()

    def hello(device):
        pl.semaphore_signal(barrier, inc=1, device_id=device, device_id_type=MESH)

    for d in range(1, NY):
        hello({"ray": lax.rem(y + d, NY)})
    hello(at(x, z, 1 - core))
    for d in range(1, NZ):
        hello(at(x, lax.rem(z + d, NZ), core))
    for d in range(1, NX):
        hello(at(lax.rem(x + d, NX), z, core))
    small = [
        pltpu.make_async_copy(src, dst, in_sem.at[i])
        for i, (src, dst) in enumerate(
            [
                (w1_hbm, w1), (w2_hbm, w2), (wo_hbm, wo), (index_hbm.at[0], index),
                (step_hbm.at[0], step), (count_hbm, count),
                (bricks.at[0], table_bf.at[pl.ds(y * 128, 128)]),
            ]
        )
    ]
    def wv_copy(c):
        n = TILES // CHUNKS
        return pltpu.make_async_copy(interp.at[0, pl.ds(c * n, n)], wv.at[pl.ds(c * n, n)], wv_sem.at[c])

    for c in range(CHUNKS):
        wv_copy(c).start()

    pl.semaphore_wait(barrier, (NY - 1) + 1 + (NZ - 1) + (NX - 1))

    def y_rows(owner, first):
        return table_bf.at[pl.ds(lax.rem(owner + NY, NY) * 128 + first, 32)]

    y_plan = [(y, 0, 1), (y, 64, 3), (y, 32, 1), (y, 96, 3), (y, 64, 1), (y, 0, 3), (y, 96, 1), (y, 32, 3)]
    y_plan += [(y - 1, 0, 1), (y + 1, 64, 3), (y - 1, 32, 1), (y + 1, 96, 3)]

    def y_copy(n):
        owner, first, to = y_plan[n]
        return pltpu.make_async_remote_copy(
            src_ref=y_rows(owner, first) if n >= 8 else bricks.at[0, pl.ds(first, 32)],
            dst_ref=y_rows(owner, first),
            send_sem=ysend_sem,
            recv_sem=yrecv_sem.at[n],
            device_id={"ray": lax.rem(y + to, NY)},
            device_id_type=MESH,
        )

    for n in range(8):
        y_copy(n).start()

    for copy in small:
        copy.start()

    for copy in small:
        copy.wait()
    w2t[...] = w2[...].astype(F32).T.astype(BF)

    for c in range(CHUNKS):
        if c in FORWARD:
            for n in range(2):
                n += 2 * FORWARD.index(c)
                y_copy(n).wait_recv()
                y_copy(8 + n).start()
        wv_copy(c).wait()

        @pl.loop(0, TILES // CHUNKS)
        def _(i):
            t = c * (TILES // CHUNKS) + i
            b = lax.rem(i, 2)
            stage[b] = wv[t].astype(F32)
            wv[t, 0:RAYS] = stage[b, pl.ds(0, RAYS, stride=2), :].astype(BF)
            wv[t, RAYS : 2 * RAYS] = stage[b, pl.ds(1, RAYS, stride=2), :].astype(BF)

    half = w1[...]
    none = jnp.zeros_like(half)
    wide = [jnp.concatenate([half, none], 0), jnp.concatenate([none, half], 0)]
    flat = table.reshape(2, 4096, LANES)

    def fold(owner):
        first = pl.multiple_of(lax.rem(owner + NY, NY) * 128, 128)
        for v in range(8):
            block = table_bf[pl.ds(first, 128), v // 2 * LANES : v // 2 * LANES + LANES]
            got = jnp.dot(block, wide[v % 2], preferred_element_type=F32)
            for h in range(2):
                flat[h, pl.ds(first * 8 + v, 128, stride=8), :] = got[:, h * LANES : (h + 1) * LANES]

    for owner, arrivals in ((y, ()), (y - 1, (4, 6)), (y + 1, (5, 7)), (y + 2, (8, 9, 10, 11))):
        for n in arrivals:
            y_copy(n).wait_recv()
        fold(owner)

    def offsets(p):
        j = lax.rem(p, 4)
        return 4 + j, 3 - j

    def column(k):
        return lax.rem(x + 1 + k, NX)

    def tile(p, u, c):
        return column(p // 4) * (2 * NZ) + lax.rem(z + offsets(p)[u], NZ) * 2 + c

    def tiles(i):
        first, last = i < LEAD // 2, i >= STEPS - LEAD // 2
        a = jnp.where(first, 2 * i, jnp.where(last, 2 * i - PAIRS, i + LEAD // 2))
        b = jnp.where(first, 2 * i + 1, jnp.where(last, 2 * i - PAIRS + 1, i - LEAD // 2))
        ca = jnp.where(last, core, 1 - core)
        cb = jnp.where(first, 1 - core, core)
        return [tile(a, 0, ca), tile(a, 1, ca), tile(b, 0, cb), tile(b, 1, cb)]

    def layer1(i, h1):
        for u, t in enumerate(tiles(i)):
            ids = [index[j, t] for j in range(16)]
            g = [jnp.concatenate([table[h, b] for b in ids], 0).T for h in range(2)]
            g = jnp.concatenate(g, 0).astype(BF)
            r = lax.dot_general(g, wv[t], (((1,), (1,)), ((), ())), preferred_element_type=F32)
            h1[u * 256 : (u + 1) * 256] = jnp.maximum(r.astype(BF), 0)

    def layer2(h1, h2):
        for u in range(GROUP):
            r = jnp.dot(w2t[...], h1[u * 256 : (u + 1) * 256], preferred_element_type=F32)
            h2[u * 256 : (u + 1) * 256] = jnp.maximum(r.astype(BF), 0)

    def shade(h2, u, t):
        o = jnp.dot(wo[...], h2[u * 256 : (u + 1) * 256], preferred_element_type=F32)
        lanes = pl.ds(pl.multiple_of(t * RAYS, RAYS), RAYS)
        n = count[0:1, lanes]
        tau0 = softplus(o[32:33, :RAYS]) * step[0:1, lanes] * jnp.where(n > 0, 1.0, 0.0)
        tau1 = softplus(o[32:33, RAYS:]) * step[1:2, lanes] * jnp.where(n > 1, 1.0, 0.0)
        a0 = jnp.exp(-tau0)
        a1 = jnp.exp(-tau1)
        color = o[0:32, :RAYS] * (1.0 - a0) + o[0:32, RAYS:] * (a0 * (1.0 - a1))
        return color, a0 * a1

    def shade_other(p, h2, u):
        for v in range(2):
            put(csend.at[p, v], *shade(h2, u + v, tile(p, v, 1 - core)))

    def shade_own(p, h2, u):
        front = core == 0
        for v in range(2):
            color, light = shade(h2, u + v, tile(p, v, core))
            left, right, tleft, tright = get(crecv.at[p, v])
            piece = []
            for a, ta, b, tb in (
                (color[:, :LANES], light[:, :LANES], left, tleft),
                (color[:, LANES:], light[:, LANES:], right, tright),
            ):
                piece.append(a * jnp.where(front, 1.0, tb) + b * jnp.where(front, ta, 1.0))
                piece.append(ta * tb)
            off = offsets(p)[v]
            code(zsend.at[p // 4, off], piece[0::2] + piece[1::2])

    def c_copy(n):
        return pltpu.make_async_remote_copy(
            src_ref=csend.at[pl.ds(2 * n, 2)],
            dst_ref=crecv.at[pl.ds(2 * n, 2)],
            send_sem=cs_sem,
            recv_sem=cr_sem.at[n],
            device_id=at(x, z, 1 - core),
            device_id_type=MESH,
        )

    def wait_for(ref, sem):
        pltpu.make_async_copy(ref, ref, sem).wait()

    def z_copy(k, off):
        return pltpu.make_async_remote_copy(
            src_ref=zsend.at[k, off],
            dst_ref=zrecv.at[k, z],
            send_sem=zs_sem,
            recv_sem=zr_sem.at[k],
            device_id=at(x, lax.rem(z + off, NZ), core),
            device_id_type=MESH,
        )

    def code(ref, piece):
        row = lax.broadcasted_iota(jnp.int32, (16, LANES), 0)
        kind = jnp.bitwise_and(row, 3)
        top = []
        for h in range(2):
            most = jnp.maximum(jnp.max(jnp.abs(piece[h]), axis=0, keepdims=True), 1e-30)
            ref[32 * h : 32 * h + 32, :] = (piece[h] * (TOP / most)).astype(jnp.int32).astype(jnp.int16)
            top.append(most * (1.0 / TOP))
        value = jnp.where(
            kind < 2,
            jnp.where(kind == 0, piece[2], piece[3]),
            jnp.where(kind == 2, top[0], top[1]),
        )
        fixed = (jnp.log(jnp.maximum(value, 1e-37)) * FINE).astype(jnp.int32)
        parts = jnp.where(row < 4, jnp.right_shift(fixed, 15), jnp.bitwise_and(fixed, 32767))
        ref[64:80, :] = jnp.where(row < 8, parts, 0).astype(jnp.int16)

    def decode(ref):
        parts = ref[64:80, :].astype(jnp.int32)
        value = jnp.exp(parts[0:4].astype(F32) * (32768.0 / FINE) + parts[4:8].astype(F32) * (1.0 / FINE))
        halves = [
            ref[32 * h : 32 * h + 32, :].astype(jnp.int32).astype(F32) * value[2 + h : 3 + h] for h in range(2)
        ]
        return halves[0], halves[1], value[0:1], value[1:2]

    def x_copy(k):
        return pltpu.make_async_remote_copy(
            src_ref=xsend.at[k, pl.ds(0, USED)],
            dst_ref=xrecv.at[x, pl.ds(0, USED)],
            send_sem=xs_sem,
            recv_sem=xr_sem,
            device_id=at(column(k), z, core),
            device_id_type=MESH,
        )

    def send_own(p):
        k, off = p // 4, offsets(p)
        z_copy(k, off[0]).start()
        own = lax.rem(p, 4) == 3

        @pl.when(own)
        def _():
            zrecv[k, z] = zsend[k, 0]

        @pl.when(jnp.logical_not(own))
        def _():
            z_copy(k, off[1]).start()

    def merge_z(k):
        wait_for(zrecv.at[k, pl.ds(0, NZ - 1)], zr_sem.at[k])
        return ordered([decode(zrecv.at[k, s]) for s in range(NZ)])

    def hand_on(k):
        put4(xsend.at[k], merge_z(k))
        x_copy(k).start()

    def compute(i, now, before):
        layer2(before[0], before[1])
        layer1(i, now[0])

    def work(i, now, before):
        shade_other(i, now[1], 0)
        shade_own(i - 4, now[1], 2)
        compute(i, now, before)
        send_own(i - 4)

    even, odd = (h1a, h2a), (h1b, h2b)
    layer1(0, h1a)
    layer2(h1a, h2a)
    layer1(1, h1b)
    for i in range(2, 4):
        now, before = (even, odd) if i % 2 == 0 else (odd, even)
        first = 2 * (i - 2)
        for n in range(2):
            shade_other(first + n, now[1], 2 * n)
        compute(i, now, before)
        c_copy(i - 2).start()

    @pl.loop(2, STEPS // 2)
    def _(n):
        c_copy(n - 2).wait_recv()
        work(2 * n, even, odd)

        work(2 * n + 1, odd, even)
        c_copy(n).start()

    for i in range(2):
        now = even if i == 0 else odd
        first = PAIRS - LEAD + 2 * i
        c_copy(first // 2).wait_recv()
        for n in range(2):
            shade_own(first + n, now[1], 2 * n)
            if i == 1:
                send_own(first + n)
        if i == 0:
            layer2(h1b, h2b)
            for n in range(2):
                send_own(first + n)
    for k in range(3):
        hand_on(k)
    put4(xrecv.at[x], merge_z(3))
    wait_for(xrecv.at[pl.ds(0, NX - 1), pl.ds(0, USED)], xr_sem)
    left, right, tleft, tright = ordered([get(xrecv.at[s]) for s in range(NX)])
    color_out[:, :LANES] = left
    color_out[:, LANES:] = right
    light_out[:, :LANES] = tleft
    light_out[:, LANES:] = tright

    wait_for(table_bf.at[pl.ds(0, 384)], ysend_sem)
    wait_for(csend, cs_sem)
    wait_for(zsend.at[:, pl.ds(1, NZ - 1)], zs_sem)
    wait_for(xsend.at[pl.ds(0, NX - 1), pl.ds(0, USED)], xs_sem)


def shards(bricks, pair_index, interp_weight, step_len, sample_count, w_first, w_second, w_out):
    part = functools.partial(pltpu.VMEM, dtype=F32)
    dma = pltpu.SemaphoreType.DMA
    color, light = pl.pallas_call(
        kernel,
        out_shape=(jax.ShapeDtypeStruct((32, RAYS), F32), jax.ShapeDtypeStruct((1, RAYS), F32)),
        in_specs=[pl.BlockSpec(memory_space=pltpu.HBM)] * 8,
        out_specs=[pl.BlockSpec(memory_space=pltpu.VMEM)] * 2,
        scratch_shapes=[
            pltpu.VMEM((512, 512), BF),
            pltpu.SMEM((16, 64), jnp.int32),
            pltpu.VMEM((TILES, 2 * RAYS, LANES), BF),
            pltpu.VMEM((2, TILES * RAYS), F32),
            pltpu.VMEM((1, TILES * RAYS), jnp.int32),
            pltpu.VMEM((64, 256), BF),
            pltpu.VMEM((256, 256), BF),
            pltpu.VMEM((33, 256), BF),
            pltpu.VMEM((256, 256), BF),
            pltpu.VMEM((2, 2 * RAYS, LANES), F32),
            pltpu.VMEM((2, 512, 8, LANES), F32),
        ]
        + [pltpu.VMEM((GROUP * 256, 512), BF)] * 4
        + [part((PAIRS, 2, ROWS, LANES))] * 2
        + [pltpu.VMEM((NX, NZ, 80, LANES), jnp.int16)] * 2
        + [part((NX, ROWS, LANES))] * 2
        + [dma((7,)), dma((CHUNKS,)), dma, dma((12,)), dma, dma((PAIRS // 2,))]
        + [dma, dma((NX,)), dma, dma],
        compiler_params=pltpu.CompilerParams(
            collective_id=0, has_side_effects=True, vmem_limit_bytes=62 * 2**20
        ),
        name="render",
    )(
        bricks,
        jnp.swapaxes(pair_index, 1, 2),
        interp_weight,
        step_len,
        sample_count,
        w_first,
        w_second,
        w_out.T,
    )
    return color, light.reshape(RAYS)


def solution(mesh):
    return jax.shard_map(
        shards,
        mesh=mesh,
        in_specs=(
            P("region", "ray", None),
            P("region", "ray", None),
            P("region", "ray", None, None),
            P("region", None, "ray"),
            P("region", "ray"),
            P(),
            P(),
            P(),
        ),
        out_specs=(P(None, ("ray", "region")), P(("ray", "region"))),
        check_vma=False,
    )
```
